32 devices in a mesh: groups: 2 (over x), ctx: 8 (over z, y), tp: 2 (over core).
Axes of the slice: x: 2, y: 2, z: 4, core: 2. Of those that a mesh axis runs over, the one named last changes fastest.
Arguments:
- queries: bfloat16 [3072, 4096], P(('groups', 'ctx'), 'tp'), parts along dimension 0, may hold values from -400 to 400
- keys: bfloat16 [3072, 512], P(('groups', 'ctx'), 'tp'), parts along dimension 0, may hold values from -400 to 400
- values: bfloat16 [3072, 512], P(('groups', 'ctx'), 'tp'), parts along dimension 0, may hold values from -6 to 6
- q_gain: float32 [128], replicated, may hold values from 1 to 5
- k_gain: float32 [128], replicated, may hold values from 1 to 5
- counts: int32 [16], P('groups'), parts along dimension 0, may hold values from 48 to 192, as said below
Outputs:
- attended: bfloat16 [3072, 4096], P(('groups', 'ctx'), 'tp'), parts along dimension 0
The draws below stay inside these ranges and needn't reach their ends.
There are 2 independent parts, one for each index of `groups`. The reference program is written for one: setup_inputs(seed, part) draws one part's arguments, and reference() takes and returns one part's arrays. A program takes and returns all parts, laid end to end along the dimension named above; an argument that names none is the same for every part. Nothing has to cross between parts.
Inputs may be any that keep to these rules, and one draw needn't show every extreme that they name: `counts`: some block has all 192 tokens live and some block only 48.
All inputs are finite; a program needn't handle non-finite values.
Results may differ from the reference program's by a relative error of at most 0.004.
The reference program's roundings to bfloat16 on the way count: a program that leaves them out, or rounds other values in their place, can miss the bound.
Values may be sent and summed in bfloat16 or wider, within the bound.
A program may use at most 64 MiB of HBM per device.

```python
import jax
import jax.numpy as jnp
from jax import lax

HD = 128
HEADS = 32
KV_HEADS = 4
TOK_DEV = 192
GROUP = 8
SEQ = 1536
N_CTX = 8


def scaled_normal(key, row_count, col_count):
    entries = jnp.clip(jax.random.normal(jax.random.fold_in(key, 11), (row_count, col_count)), -4.0, 4.0)
    row_scale = jnp.exp(jax.random.uniform(jax.random.fold_in(key, 12), (row_count, 1), minval=0.0, maxval=jnp.log(10.0)))
    col_scale = jnp.exp(jax.random.uniform(jax.random.fold_in(key, 13), (1, col_count), minval=0.0, maxval=jnp.log(10.0)))
    return entries * row_scale * col_scale


def draw_queries(key, part):
    key = jax.random.fold_in(key, 1)
    drawn = scaled_normal(key, SEQ, HEADS * HD).reshape(SEQ, HEADS, HD)
    return drawn.reshape(SEQ, HEADS * HD).astype(jnp.bfloat16)


def draw_keys(key, part):
    key = jax.random.fold_in(key, 2)
    drawn = scaled_normal(key, SEQ, KV_HEADS * HD).reshape(SEQ, KV_HEADS, HD)
    return drawn.reshape(SEQ, KV_HEADS * HD).astype(jnp.bfloat16)


def draw_q_gain(key, part):
    key = jax.random.fold_in(key, 3)
    return jnp.exp(jax.random.uniform(key, (HD,), minval=0.0, maxval=jnp.log(2.5)))


def draw_k_gain(key, part):
    key = jax.random.fold_in(key, 4)
    return jnp.exp(jax.random.uniform(key, (HD,), minval=0.0, maxval=jnp.log(2.5)))


def draw_counts(key, part):
    key = jax.random.fold_in(key, 5)
    counts_base = jax.random.randint(jax.random.fold_in(key, 1), (N_CTX,), TOK_DEV // 4, TOK_DEV + 1)
    full_shard = jax.random.randint(jax.random.fold_in(key, 2), (), 0, N_CTX)
    low_shard = (full_shard + 1 + jax.random.randint(jax.random.fold_in(key, 3), (), 0, N_CTX - 1)) % N_CTX
    shard_index = jnp.arange(N_CTX, dtype=jnp.int32)
    counts_base = jnp.where(shard_index == low_shard, TOK_DEV // 4, counts_base)
    return jnp.where(shard_index == full_shard, TOK_DEV, counts_base).astype(jnp.int32)


def shard_levels(key, dims, shards, least, high):
    def one(dim, blocks):
        draws = jax.random.uniform(jax.random.fold_in(jax.random.fold_in(key, 6), dim), (blocks,), jnp.float32, least / len(shards), high / len(shards))
        return jnp.repeat(jnp.exp(draws), dims[dim] // blocks).reshape((-1,) + (1,) * (len(dims) - dim - 1))

    level = one(*shards[0])
    for cut in shards[1:]:
        level = level * one(*cut)
    return level


def scatter_about(own_key, extent, scale, limit, pieces=(), kind=jnp.bfloat16):
    values = scale * jax.random.normal(own_key, extent, jnp.float32)
    if pieces:
        values = values * shard_levels(own_key, extent, pieces, -0.22, 0.18)
    return jnp.clip(values, -limit, limit).astype(kind)


def setup_inputs(seed: int = 0, part: int = 0) -> dict:
    arg_keys = jax.random.split(jax.random.key(seed), 7)
    part_keys = jax.random.split(jax.random.fold_in(arg_keys[6], part), 7)
    queries = draw_queries(jax.random.fold_in(jax.random.fold_in(arg_keys[6], part), 71), part)
    keys = draw_keys(jax.random.fold_in(jax.random.fold_in(arg_keys[6], part), 71), part)
    values = scatter_about(part_keys[2], (SEQ, KV_HEADS * HD), 1.0, 6.0, ((0, 8), (1, 2)))
    q_gain = draw_q_gain(jax.random.fold_in(arg_keys[6], 71), part)
    k_gain = draw_k_gain(jax.random.fold_in(arg_keys[6], 71), part)
    counts = draw_counts(jax.random.fold_in(jax.random.fold_in(arg_keys[6], part), 71), part)
    return dict(queries=queries, keys=keys, values=values, q_gain=q_gain, k_gain=k_gain, counts=counts)


def rope_tables(positions, head_width):
    frequency = jnp.power(jnp.float32(1000000.0), -jnp.arange(0, head_width, 2).astype(jnp.float32) / head_width)
    angles = positions.astype(jnp.float32)[:, None] * frequency[None, :]
    cosine_table = jnp.cos(angles)
    sine_table = jnp.sin(angles)
    return (jnp.concatenate([cosine_table, cosine_table], 1), jnp.concatenate([sine_table, sine_table], 1))

def norm_rope(inputs, gain, positions, head_width):
    row_count = inputs.shape[0]
    head_count = inputs.shape[1] // head_width
    normed = inputs.astype(jnp.float32).reshape(row_count, head_count, head_width)
    normed = normed * lax.rsqrt(lax.optimization_barrier(jnp.mean(normed * normed, -1, keepdims=True)) + 1e-06) * gain
    cosine_table, sine_table = rope_tables(positions, head_width)
    turned = jnp.concatenate([-normed[..., head_width // 2:], normed[..., :head_width // 2]], -1)
    rotated = normed * cosine_table[:, None, :] + turned * sine_table[:, None, :]
    return rotated.astype(jnp.bfloat16)

def reference(queries, keys, values, q_gain, k_gain, counts):
    positions = jnp.arange(SEQ, dtype=jnp.int32)
    is_live = positions % TOK_DEV < counts[positions // TOK_DEV]
    q_ready = norm_rope(queries, q_gain, positions, HD).reshape(SEQ, KV_HEADS, GROUP, HD)
    k_float = norm_rope(keys, k_gain, positions, HD).astype(jnp.float32)
    value_rows = values.reshape(SEQ, KV_HEADS, HD).astype(jnp.float32)
    score_scale = HD ** (-0.5)

    def attend_block(scan_item):
        query_block, query_pos, query_live = scan_item
        scores = jnp.einsum('qkgd,skd->kgqs', query_block.astype(jnp.float32), k_float) * score_scale
        allowed = is_live[None, :] & (positions[None, :] <= query_pos[:, None])
        scores = jnp.where(allowed[None, None], scores, -1e+30)
        row_max = lax.optimization_barrier(jnp.max(scores, -1, keepdims=True))
        weights = jnp.where(allowed[None, None], jnp.exp(scores - row_max), 0.0)
        row_total = lax.optimization_barrier(jnp.sum(weights, -1))
        summed = jnp.einsum('kgqs,skd->kgqd', weights.astype(jnp.bfloat16).astype(jnp.float32), value_rows)
        summed = summed / row_total[..., None]
        summed = jnp.transpose(summed, (2, 0, 1, 3)).reshape(TOK_DEV, HEADS * HD)
        return jnp.where(query_live[:, None], summed, 0.0).astype(jnp.bfloat16)
    blocks = lax.map(attend_block, (q_ready.reshape(N_CTX, TOK_DEV, KV_HEADS, GROUP, HD), positions.reshape(N_CTX, TOK_DEV), is_live.reshape(N_CTX, TOK_DEV)))
    return blocks.reshape(SEQ, HEADS * HD)
```

```python
import functools
import math

import jax
import jax.numpy as jnp
import numpy as np
from jax import lax
from jax.experimental import pallas as pl
from jax.experimental.pallas import tpu as pltpu
from jax.sharding import PartitionSpec as P

MESH = pl.DeviceIdType.MESH
FAR = -1e30
THETA = 1000000.0
ROWS = 768


def rope_constants(shards, shard_rows, width):
    frequency = THETA ** (-np.arange(0, width, 2, dtype=np.float64) / width)
    frequency = np.concatenate([frequency, frequency])
    inner = np.arange(shard_rows)[:, None] * frequency[None, :]
    start = (np.arange(shards) * shard_rows)[:, None] * frequency[None, :]
    inner = np.stack([np.cos(inner), np.sin(inner)]).astype(np.float32)
    start = np.stack([np.cos(start), np.sin(start)], 1).astype(np.float32)
    return inner, start


def kernel(
    shards,
    width,
    q_in,
    k_in,
    v_in,
    q_gain,
    k_gain,
    counts,
    inner,
    start,
    out,
    kv,
    q_wide,
    top,
    total,
    summed,
    k_table,
    send_up,
    send_over,
    recv,
):
    shard_rows = q_in.shape[0]
    heads = q_in.shape[1] // width
    kv_heads = k_in.shape[1] // width
    group = heads // kv_heads
    pair_rows = 2 * shard_rows
    levels = shards // 2
    batch = max(1, min(group, ROWS // shard_rows))
    half = width // 2
    bf16, f32 = jnp.bfloat16, jnp.float32

    me = lax.axis_index("ctx")
    level = me // 2
    side = lax.rem(me, 2)
    over = me + 1 - 2 * side
    up = lax.rem(me + 2, shards)
    down = lax.rem(me - 2 + shards, shards)
    not_last = level < levels - 1
    not_first = level > 0

    barrier = pltpu.get_barrier_semaphore()
    pl.semaphore_signal(barrier, inc=1, device_id={"ctx": over}, device_id_type=MESH)

    @pl.when(not_last)
    def _():
        pl.semaphore_signal(barrier, inc=1, device_id={"ctx": up}, device_id_type=MESH)

    @pl.when(not_first)
    def _():
        pl.semaphore_signal(barrier, inc=1, device_id={"ctx": down}, device_id_type=MESH)

    def place(block, part):
        offset = pl.multiple_of(lax.rem(block, 2) * shard_rows, shard_rows)
        return kv.at[block // 2, part, pl.ds(offset, shard_rows), :]

    def copy(block, part, sems, target):
        return pltpu.make_async_remote_copy(
            src_ref=place(block, part),
            dst_ref=place(block, part),
            send_sem=sems.at[block, part],
            recv_sem=recv.at[block, part],
            device_id={"ctx": target},
            device_id_type=MESH,
        )

    def to_up(block, part):
        return copy(block, part, send_up, up)

    def to_over(block, part):
        return copy(block, part, send_over, over)

    c0 = start[me, 0:1, :]
    s0 = start[me, 1:2, :]
    ci = inner[0]
    si = inner[1]
    cosine = c0 * ci - s0 * si
    sine = s0 * ci + c0 * si
    lane = lax.broadcasted_iota(jnp.int32, (1, width), 1)
    sine = jnp.where(lane < half, -sine, sine)

    def tables(gain):
        g = gain[...]
        return cosine * g, sine * pltpu.roll(g, half, 1)

    def ready(x, by_cos, by_sin):
        x = x.astype(f32)
        scale = lax.rsqrt(jnp.mean(x * x, -1, keepdims=True) + 1e-06)
        return ((x * by_cos + pltpu.roll(x, half, 1) * by_sin) * scale).astype(bf16)

    live = lax.broadcasted_iota(jnp.int32, (shard_rows, width), 0) < counts[me]
    by_cos, by_sin = tables(k_gain)
    own = pl.multiple_of(side * shard_rows, shard_rows)
    for h in range(kv_heads):
        cut = slice(h * width, (h + 1) * width)
        k = ready(k_in[:, cut], by_cos, by_sin).astype(f32)
        k = jnp.where(live, k, k[0:1, :])
        kv[level, 0, pl.ds(own, shard_rows), cut] = k.astype(bf16)
        v = jnp.where(live, v_in[:, cut].astype(f32), 0.0)
        kv[level, 1, pl.ds(own, shard_rows), cut] = v.astype(bf16)

    @pl.when(side == 0)
    def _():
        for part in range(2):
            kv[level, part, shard_rows:, :] = jnp.zeros((shard_rows, kv_heads * width), bf16)

    pl.semaphore_wait(
        barrier, 1 + jnp.where(not_last, 1, 0) + jnp.where(not_first, 1, 0)
    )

    for part in range(2):

        @pl.when(side == 0)
        def _():
            to_over(me, part).start()

        @pl.when(not_last)
        def _():
            to_up(me, part).start()

    by_cos, by_sin = tables(q_gain)
    k_table[0] = by_cos
    k_table[1] = by_sin
    score_scale = math.log2(math.e) / math.sqrt(width)
    for h in range(heads):
        q = ready(q_in[:, h * width : (h + 1) * width], k_table[0], k_table[1])
        q = q.astype(f32) * score_scale
        high = q.astype(bf16)
        low = (q - high.astype(f32)).astype(bf16)
        q_wide[h, :, :width] = high
        q_wide[h, :, width:] = low

    @pl.when(side == 1)
    def _():
        to_over(me - 1, 0).wait_recv()

        @pl.when(not_last)
        def _():
            to_up(me - 1, 0).start()

    def relay(pair):
        block = 2 * pair + side
        for part in range(2):
            to_up(block, part).wait_recv()

            @pl.when(not_last)
            def _():
                to_up(block, part).start()

            if part == 0:

                @pl.when((side == 1) | (pair < level - 1))
                def _():
                    to_over(block, part).start()

            else:
                to_over(block, part).start()

    def attend(pair, first):
        blocks = [2 * pair, 2 * pair + 1]
        row = lax.broadcasted_iota(jnp.int32, (shard_rows, width), 0)
        alive = jnp.concatenate(
            [jnp.where(row < counts[b], 1.0, 0.0).astype(bf16) for b in blocks], 0
        )
        for h in range(kv_heads):
            cut = slice(h * width, (h + 1) * width)
            k = kv[pair, 0, :, cut]
            v = kv[pair, 1, :, cut]
            k2 = jnp.concatenate([k, k], 1)
            v2 = jnp.concatenate([v, alive], 1)

            @pl.loop(0, group // batch)
            def _(i):
                at = h * group + i * batch
                rows = batch * shard_rows
                q = q_wide[pl.ds(at, batch)].reshape(rows, 2 * width)
                s = lax.dot_general(
                    q, k2, (((1,), (1,)), ((), ())), preferred_element_type=f32
                )
                if first:
                    q_at = lax.broadcasted_iota(jnp.int32, (batch, shard_rows, pair_rows), 1)
                    k_at = lax.broadcasted_iota(jnp.int32, (batch, shard_rows, pair_rows), 2)
                    seen = (k_at <= q_at + side * shard_rows).reshape(rows, pair_rows)
                    s = jnp.where(seen, s, FAR)
                parts = [s[:, j : j + width] for j in range(0, pair_rows, width)]
                peak = functools.reduce(jnp.maximum, parts)
                peak = jnp.max(peak, -1, keepdims=True)
                state = pl.ds(pl.multiple_of(at * shard_rows, shard_rows), rows)
                if first:
                    new = jnp.broadcast_to(peak, (rows, width))
                else:
                    old = top[state, :]
                    new = jnp.maximum(old, peak)
                weights = jnp.concatenate(
                    [jnp.exp2(part - new).astype(bf16) for part in parts], 1
                )
                o = jnp.dot(weights, v2, preferred_element_type=f32)
                top[state, :] = new
                if first:
                    summed[state, :] = o[:, :width]
                    total[state, :] = o[:, width:]
                else:
                    rescale = jnp.exp2(old - new)
                    summed[state, :] = summed[state, :] * rescale + o[:, :width]
                    total[state, :] = total[state, :] * rescale + o[:, width:]

    def await_over(pair):
        block = 2 * pair + 1 - side
        for part in range(2):
            to_over(block, part).wait_recv()

    @pl.when(not_first)
    def _():
        relay(level - 1)

    @pl.when(side == 1)
    def _():
        to_over(me - 1, 1).wait_recv()

    attend(level, True)

    @pl.loop(0, level)
    def _(step):
        pair = level - 1 - step

        @pl.when(pair > 0)
        def _():
            relay(pair - 1)

        await_over(pair)
        attend(pair, False)

    for h in range(heads):
        state = slice(h * shard_rows, (h + 1) * shard_rows)
        o = summed[state, :] / total[state, :]
        out[:, h * width : (h + 1) * width] = jnp.where(live, o, 0.0).astype(bf16)

    for part in range(2):

        @pl.when(side == 0)
        def _():
            to_over(me, part).wait_send()

        @pl.when(not_last)
        def _():
            to_up(me, part).wait_send()

    @pl.when((side == 1) & not_last)
    def _():
        to_up(me - 1, 0).wait_send()

    @pl.loop(0, level)
    def _(pair):
        block = 2 * pair + side
        for part in range(2):

            @pl.when(not_last)
            def _():
                to_up(block, part).wait_send()

            if part == 0:

                @pl.when((side == 1) | (pair < level - 1))
                def _():
                    to_over(block, part).wait_send()

            else:
                to_over(block, part).wait_send()


def local(shards, queries, keys, values, q_gain, k_gain, counts):
    shard_rows = queries.shape[0]
    width = q_gain.shape[0]
    heads = queries.shape[1] // width
    inner, start = rope_constants(shards, shard_rows, width)
    vmem = pl.BlockSpec(memory_space=pltpu.VMEM)
    state = pltpu.VMEM((heads * shard_rows, width), jnp.float32)
    return pl.pallas_call(
        functools.partial(kernel, shards, width),
        out_shape=jax.ShapeDtypeStruct(queries.shape, jnp.bfloat16),
        in_specs=[vmem] * 5 + [pl.BlockSpec(memory_space=pltpu.SMEM)] + [vmem] * 2,
        out_specs=vmem,
        scratch_shapes=[
            pltpu.VMEM((shards // 2, 2, 2 * shard_rows, keys.shape[1]), jnp.bfloat16),
            pltpu.VMEM((heads, shard_rows, 2 * width), jnp.bfloat16),
            state,
            state,
            state,
            pltpu.VMEM((2, shard_rows, width), jnp.float32),
            pltpu.SemaphoreType.DMA((shards, 2)),
            pltpu.SemaphoreType.DMA((shards, 2)),
            pltpu.SemaphoreType.DMA((shards, 2)),
        ],
        compiler_params=pltpu.CompilerParams(
            collective_id=0, has_side_effects=True, vmem_limit_bytes=48 * 2**20
        ),
        name="attend",
    )(
        queries,
        keys,
        values,
        q_gain.reshape(1, width),
        k_gain.reshape(1, width),
        counts,
        jnp.asarray(inner),
        jnp.asarray(start),
    )


def solution(mesh):
    in_specs = (
        P(("groups", "ctx"), "tp"),
        P(("groups", "ctx"), "tp"),
        P(("groups", "ctx"), "tp"),
        P(),
        P(),
        P("groups"),
    )
    out_specs = P(("groups", "ctx"), "tp")
    return jax.shard_map(
        functools.partial(local, mesh.shape["ctx"]),
        mesh=mesh,
        in_specs=in_specs,
        out_specs=out_specs,
        check_vma=False,
    )
```

```python
import functools
import math

import jax
import jax.numpy as jnp
import numpy as np
from jax import lax
from jax.experimental import pallas as pl
from jax.experimental.pallas import tpu as pltpu
from jax.sharding import PartitionSpec as P

MESH = pl.DeviceIdType.MESH
FAR = -1e30
THETA = 1000000.0
ROWS = 384


def rope_constants(shards, shard_rows, width):
    frequency = THETA ** (-np.arange(0, width, 2, dtype=np.float64) / width)
    frequency = np.concatenate([frequency, frequency])
    inner = np.arange(shard_rows)[:, None] * frequency[None, :]
    start = (np.arange(shards) * shard_rows)[:, None] * frequency[None, :]
    inner = np.stack([np.cos(inner), np.sin(inner)]).astype(np.float32)
    start = np.stack([np.cos(start), np.sin(start)], 1).astype(np.float32)
    return inner, start


def kernel(
    shards,
    width,
    q_hbm,
    k_hbm,
    v_hbm,
    q_gain_hbm,
    k_gain_hbm,
    counts,
    inner_hbm,
    start_hbm,
    out,
    q_in,
    k_in,
    v_in,
    q_gain,
    k_gain,
    inner,
    start,
    kv,
    q_wide,
    top,
    total,
    summed,
    k_table,
    send_up,
    send_over,
    recv,
    fetched,
):
    shard_rows = q_in.shape[0]
    heads = q_in.shape[1] // width
    kv_heads = k_in.shape[1] // width
    group = heads // kv_heads
    pair_rows = 2 * shard_rows
    levels = shards // 2
    batch = max(1, min(group, ROWS // shard_rows))
    half = width // 2
    bf16, f32 = jnp.bfloat16, jnp.float32

    me = lax.axis_index("ctx")
    level = me // 2
    side = lax.rem(me, 2)
    over = me + 1 - 2 * side
    up = lax.rem(me + 2, shards)
    down = lax.rem(me - 2 + shards, shards)
    not_last = level < levels - 1
    not_first = level > 0

    fetches = [
        pltpu.make_async_copy(source, target, fetched.at[i])
        for i, (source, target) in enumerate(
            [
                (k_hbm, k_in),
                (inner_hbm, inner),
                (start_hbm.at[me], start),
                (k_gain_hbm, k_gain),
                (v_hbm, v_in),
                (q_gain_hbm, q_gain),
                (q_hbm, q_in),
            ]
        )
    ]
    for fetch in fetches:
        fetch.start()

    barrier = pltpu.get_barrier_semaphore()
    pl.semaphore_signal(barrier, inc=1, device_id={"ctx": over}, device_id_type=MESH)

    @pl.when(not_last)
    def _():
        pl.semaphore_signal(barrier, inc=1, device_id={"ctx": up}, device_id_type=MESH)

    @pl.when(not_first)
    def _():
        pl.semaphore_signal(barrier, inc=1, device_id={"ctx": down}, device_id_type=MESH)

    def place(block, part):
        offset = pl.multiple_of(lax.rem(block, 2) * shard_rows, shard_rows)
        return kv.at[block // 2, part, pl.ds(offset, shard_rows), :]

    def copy(block, part, sems, target):
        return pltpu.make_async_remote_copy(
            src_ref=place(block, part),
            dst_ref=place(block, part),
            send_sem=sems.at[block, part],
            recv_sem=recv.at[block, part],
            device_id={"ctx": target},
            device_id_type=MESH,
        )

    def to_up(block, part):
        return copy(block, part, send_up, up)

    def to_over(block, part):
        return copy(block, part, send_over, over)

    for fetch in fetches[:5]:
        fetch.wait()
    c0 = start[0:1, :]
    s0 = start[1:2, :]
    ci = inner[0]
    si = inner[1]
    cosine = c0 * ci - s0 * si
    sine = s0 * ci + c0 * si
    lane = lax.broadcasted_iota(jnp.int32, (1, width), 1)
    sine = jnp.where(lane < half, -sine, sine)

    def tables(gain):
        g = gain[...]
        return cosine * g, sine * pltpu.roll(g, half, 1)

    def ready(x, by_cos, by_sin):
        x = x.astype(f32)
        scale = lax.rsqrt(jnp.mean(x * x, -1, keepdims=True) + 1e-06)
        return ((x * by_cos + pltpu.roll(x, half, 1) * by_sin) * scale).astype(bf16)

    live = lax.broadcasted_iota(jnp.int32, (shard_rows, width), 0) < counts[me]
    by_cos, by_sin = tables(k_gain)
    own = pl.multiple_of(side * shard_rows, shard_rows)
    for h in range(kv_heads):
        cut = slice(h * width, (h + 1) * width)
        k = ready(k_in[:, cut], by_cos, by_sin).astype(f32)
        k = jnp.where(live, k, k[0:1, :])
        kv[level, 0, pl.ds(own, shard_rows), cut] = k.astype(bf16)
        v = jnp.where(live, v_in[:, cut].astype(f32), 0.0)
        kv[level, 1, pl.ds(own, shard_rows), cut] = v.astype(bf16)

    @pl.when(side == 0)
    def _():
        for part in range(2):
            kv[level, part, shard_rows:, :] = jnp.zeros((shard_rows, kv_heads * width), bf16)

    pl.semaphore_wait(
        barrier, 1 + jnp.where(not_last, 1, 0) + jnp.where(not_first, 1, 0)
    )

    for part in range(2):

        @pl.when(side == 0)
        def _():
            to_over(me, part).start()

        @pl.when(not_last)
        def _():
            to_up(me, part).start()

    for fetch in fetches[5:]:
        fetch.wait()
    by_cos, by_sin = tables(q_gain)
    k_table[0] = by_cos
    k_table[1] = by_sin
    score_scale = math.log2(math.e) / math.sqrt(width)
    for h in range(heads):
        q = ready(q_in[:, h * width : (h + 1) * width], k_table[0], k_table[1])
        q = q.astype(f32) * score_scale
        high = q.astype(bf16)
        low = (q - high.astype(f32)).astype(bf16)
        at = (h % group) * shard_rows
        q_wide[h // group, at : at + shard_rows, :width] = high
        q_wide[h // group, at : at + shard_rows, width:] = low

    def relay(pair):
        block = 2 * pair + side
        for part in range(2):
            to_up(block, part).wait_recv()

            @pl.when(not_last)
            def _():
                to_up(block, part).start()

            if part == 0:

                @pl.when((side == 1) | (pair > 0))
                def _():
                    to_over(block, part).start()

            else:
                to_over(block, part).start()

    def detour():
        @pl.when(side == 1)
        def _():
            @pl.when(not_first)
            def _():
                to_up(0, 0).wait_recv()

            @pl.when(level == 0)
            def _():
                to_over(0, 0).wait_recv()

            @pl.when(not_last)
            def _():
                to_up(0, 0).start()

    def attend(pair, first):
        blocks = [2 * pair, 2 * pair + 1]
        row = lax.broadcasted_iota(jnp.int32, (shard_rows, width), 0)
        alive = jnp.concatenate(
            [jnp.where(row < counts[b], 1.0, 0.0).astype(bf16) for b in blocks], 0
        )
        if first:
            q_at = lax.broadcasted_iota(jnp.int32, (shard_rows, pair_rows), 0)
            k_at = lax.broadcasted_iota(jnp.int32, (shard_rows, pair_rows), 1)
            seen = k_at <= q_at + side * shard_rows
            seen = jnp.concatenate([seen] * batch, 0) if batch > 1 else seen

        @pl.loop(0, kv_heads)
        def _(h):
            cut = pl.ds(pl.multiple_of(h * width, width), width)
            k = kv[pair, 0, :, cut]
            v = kv[pair, 1, :, cut]
            k2 = jnp.concatenate([k, k], 1)
            v2 = jnp.concatenate([v, alive], 1)
            rows = batch * shard_rows

            def scores(i):
                q = q_wide[h, pl.ds(i * rows, rows), :]
                return lax.dot_general(
                    q, k2, (((1,), (1,)), ((), ())), preferred_element_type=f32
                )

            steps = group // batch
            coming = scores(0)
            for i in range(steps):
                s = coming
                if i + 1 < steps:
                    coming = scores(i + 1)
                if first:
                    s = jnp.where(seen, s, FAR)
                parts = [s[:, j : j + width] for j in range(0, pair_rows, width)]
                peak = functools.reduce(jnp.maximum, parts)
                peak = jnp.max(peak, -1, keepdims=True)
                state = (h, slice(i * rows, (i + 1) * rows))
                if first:
                    new = jnp.broadcast_to(peak, (rows, width))
                else:
                    old = top[state]
                    new = jnp.maximum(old, peak)
                weights = jnp.concatenate(
                    [jnp.exp2(part - new).astype(bf16) for part in parts], 1
                )
                o = jnp.dot(weights, v2, preferred_element_type=f32)
                top[state] = new
                if first:
                    summed[state] = o[:, :width]
                    total[state] = o[:, width:]
                else:
                    rescale = jnp.exp2(old - new)
                    summed[state] = summed[state] * rescale + o[:, :width]
                    total[state] = total[state] * rescale + o[:, width:]

    def await_over(pair):
        block = 2 * pair + 1 - side

        @pl.when((side == 0) | (pair > 0))
        def _():
            to_over(block, 0).wait_recv()

        to_over(block, 1).wait_recv()

    @pl.when(not_first)
    def _():
        relay(level - 1)

    @pl.when(level == 0)
    def _():
        detour()

    @pl.when(side == 1)
    def _():
        @pl.when(not_first)
        def _():
            to_over(me - 1, 0).wait_recv()

        to_over(me - 1, 1).wait_recv()

    attend(level, True)

    @pl.loop(0, level)
    def _(step):
        pair = level - 1 - step

        @pl.when(pair > 0)
        def _():
            relay(pair - 1)

        @pl.when(pair == 0)
        def _():
            detour()

        await_over(pair)
        attend(pair, False)

    for h in range(heads):
        at = (h % group) * shard_rows
        state = (h // group, slice(at, at + shard_rows))
        o = summed[state] / total[state]
        out[:, h * width : (h + 1) * width] = jnp.where(live, o, 0.0).astype(bf16)

    for part in range(2):

        @pl.when(side == 0)
        def _():
            to_over(me, part).wait_send()

        @pl.when(not_last)
        def _():
            to_up(me, part).wait_send()

    @pl.when((side == 1) & not_last)
    def _():
        to_up(0, 0).wait_send()

    @pl.loop(0, level)
    def _(pair):
        block = 2 * pair + side
        for part in range(2):

            @pl.when(not_last)
            def _():
                to_up(block, part).wait_send()

            if part == 0:

                @pl.when((side == 1) | (pair > 0))
                def _():
                    to_over(block, part).wait_send()

            else:
                to_over(block, part).wait_send()


def local(shards, queries, keys, values, q_gain, k_gain, counts):
    shard_rows = queries.shape[0]
    width = q_gain.shape[0]
    heads = queries.shape[1] // width
    inner, start = rope_constants(shards, shard_rows, width)
    vmem = pl.BlockSpec(memory_space=pltpu.VMEM)
    hbm = pl.BlockSpec(memory_space=pl.ANY)
    kv_heads = keys.shape[1] // width
    rows = heads // kv_heads * shard_rows
    state = pltpu.VMEM((kv_heads, rows, width), jnp.float32)
    return pl.pallas_call(
        functools.partial(kernel, shards, width),
        out_shape=jax.ShapeDtypeStruct(queries.shape, jnp.bfloat16),
        in_specs=[hbm] * 5 + [pl.BlockSpec(memory_space=pltpu.SMEM)] + [hbm] * 2,
        out_specs=vmem,
        scratch_shapes=[
            pltpu.VMEM(queries.shape, jnp.bfloat16),
            pltpu.VMEM(keys.shape, jnp.bfloat16),
            pltpu.VMEM(values.shape, jnp.bfloat16),
            pltpu.VMEM((1, width), jnp.float32),
            pltpu.VMEM((1, width), jnp.float32),
            pltpu.VMEM(inner.shape, jnp.float32),
            pltpu.VMEM(start.shape[1:], jnp.float32),
            pltpu.VMEM((shards // 2, 2, 2 * shard_rows, keys.shape[1]), jnp.bfloat16),
            pltpu.VMEM((kv_heads, rows, 2 * width), jnp.bfloat16),
            state,
            state,
            state,
            pltpu.VMEM((2, shard_rows, width), jnp.float32),
            pltpu.SemaphoreType.DMA((shards, 2)),
            pltpu.SemaphoreType.DMA((shards, 2)),
            pltpu.SemaphoreType.DMA((shards, 2)),
            pltpu.SemaphoreType.DMA((7,)),
        ],
        compiler_params=pltpu.CompilerParams(
            collective_id=0, has_side_effects=True, vmem_limit_bytes=60 * 2**20
        ),
        name="attend",
    )(
        queries,
        keys,
        values,
        q_gain.reshape(1, width),
        k_gain.reshape(1, width),
        counts,
        jnp.asarray(inner),
        jnp.asarray(start),
    )


def solution(mesh):
    in_specs = (
        P(("groups", "ctx"), "tp"),
        P(("groups", "ctx"), "tp"),
        P(("groups", "ctx"), "tp"),
        P(),
        P(),
        P("groups"),
    )
    out_specs = P(("groups", "ctx"), "tp")
    return jax.shard_map(
        functools.partial(local, mesh.shape["ctx"]),
        mesh=mesh,
        in_specs=in_specs,
        out_specs=out_specs,
        check_vma=False,
    )
```

```python
import functools
import math

import jax
import jax.numpy as jnp
import numpy as np
from jax import lax
from jax.experimental import pallas as pl
from jax.experimental.pallas import tpu as pltpu
from jax.sharding import PartitionSpec as P

KEYS, VALUES = 0, 1
MESH = pl.DeviceIdType.MESH
FAR = -1e30
THETA = 1000000.0
ROWS = 384


def rope_constants(shards, shard_rows, width):
    frequency = THETA ** (-np.arange(0, width, 2, dtype=np.float64) / width)
    frequency = np.concatenate([frequency, frequency])
    inner = np.arange(shard_rows)[:, None] * frequency[None, :]
    start = (np.arange(shards) * shard_rows)[:, None] * frequency[None, :]
    inner = np.stack([np.cos(inner), np.sin(inner)]).astype(np.float32)
    start = np.stack([np.cos(start), np.sin(start)], 1).astype(np.float32)
    return inner, start


def kernel(
    shards,
    width,
    q_hbm,
    k_hbm,
    v_hbm,
    q_gain_hbm,
    k_gain_hbm,
    counts_hbm,
    inner_hbm,
    start_hbm,
    out,
    q_in,
    k_in,
    q_gain,
    k_gain,
    counts,
    inner,
    start,
    kv,
    q_wide,
    top,
    total,
    summed,
    k_table,
    send_up,
    send_over,
    recv,
    fetched,
    result,
    leaving,
):
    shard_rows = q_in.shape[0]
    heads = q_in.shape[1] // width
    kv_heads = k_in.shape[1] // width
    group = heads // kv_heads
    pair_rows = 2 * shard_rows
    levels = shards // 2
    batch = max(1, min(group, ROWS // shard_rows))
    half = width // 2
    bf16, f32 = jnp.bfloat16, jnp.float32

    me = lax.axis_index("ctx")
    level = me // 2
    side = lax.rem(me, 2)
    over = me + 1 - 2 * side
    up = lax.rem(me + 2, shards)
    down = lax.rem(me - 2 + shards, shards)
    not_last = level < levels - 1
    not_first = level > 0
    own = pl.multiple_of(side * shard_rows, shard_rows)

    fetches = [
        pltpu.make_async_copy(source, target, fetched.at[i])
        for i, (source, target) in enumerate(
            [
                (k_hbm, k_in),
                (inner_hbm, inner),
                (start_hbm.at[me], start),
                (k_gain_hbm, k_gain),
                (counts_hbm, counts),
                (q_gain_hbm, q_gain),
                (q_hbm, q_in),
                (v_hbm, kv.at[level, VALUES, pl.ds(own, shard_rows), :]),
            ]
        )
    ]
    for fetch in fetches:
        fetch.start()

    barrier = pltpu.get_barrier_semaphore()
    pl.semaphore_signal(barrier, inc=1, device_id={"ctx": over}, device_id_type=MESH)

    @pl.when(not_last)
    def _():
        pl.semaphore_signal(barrier, inc=1, device_id={"ctx": up}, device_id_type=MESH)

    @pl.when(not_first)
    def _():
        pl.semaphore_signal(barrier, inc=1, device_id={"ctx": down}, device_id_type=MESH)

    def place(block, part):
        offset = pl.multiple_of(lax.rem(block, 2) * shard_rows, shard_rows)
        return kv.at[block // 2, part, pl.ds(offset, shard_rows), :]

    def copy(block, part, sems, target, source):
        return pltpu.make_async_remote_copy(
            src_ref=place(block, part) if source is None else source,
            dst_ref=place(block, part),
            send_sem=sems.at[block, part],
            recv_sem=recv.at[block, part],
            device_id={"ctx": target},
            device_id_type=MESH,
        )

    def to_up(block, part, source=None):
        return copy(block, part, send_up, up, source)

    def to_over(block, part, source=None):
        return copy(block, part, send_over, over, source)

    pl.semaphore_wait(
        barrier, 1 + jnp.where(not_last, 1, 0) + jnp.where(not_first, 1, 0)
    )

    @pl.when(side == 0)
    def _():
        to_over(me, VALUES, v_hbm).start()

    @pl.when(not_last)
    def _():
        to_up(me, VALUES, v_hbm).start()

    def send_own_keys():
        @pl.when((side == 0) | (level == 0))
        def _():
            to_over(me, KEYS).start()

        @pl.when(not_last)
        def _():
            to_up(me, KEYS).start()

    for fetch in fetches[:5]:
        fetch.wait()
    c0 = start[0:1, :]
    s0 = start[1:2, :]
    ci = inner[0]
    si = inner[1]
    cosine = c0 * ci - s0 * si
    sine = s0 * ci + c0 * si
    lane = lax.broadcasted_iota(jnp.int32, (1, width), 1)
    sine = jnp.where(lane < half, -sine, sine)

    def tables(gain):
        g = gain[...]
        return cosine * g, sine * pltpu.roll(g, half, 1)

    def ready(x, by_cos, by_sin):
        x = x.astype(f32)
        scale = lax.rsqrt(jnp.mean(x * x, -1, keepdims=True) + 1e-06)
        return ((x * by_cos + pltpu.roll(x, half, 1) * by_sin) * scale).astype(bf16)

    live = lax.broadcasted_iota(jnp.int32, (shard_rows, width), 0) < counts[me]
    by_cos, by_sin = tables(k_gain)
    for h in range(kv_heads):
        cut = slice(h * width, (h + 1) * width)
        k = ready(k_in[:, cut], by_cos, by_sin).astype(f32)
        k = jnp.where(live, k, k[0:1, :])
        kv[level, KEYS, pl.ds(own, shard_rows), cut] = k.astype(bf16)

    @pl.when(side == 0)
    def _():
        blank = jnp.zeros((shard_rows, kv_heads * width), bf16)
        kv[level, VALUES, shard_rows:, :] = blank

        @pl.when(not_first)
        def _():
            kv[level, KEYS, shard_rows:, :] = blank

    for fetch in fetches[5:7]:
        fetch.wait()
    by_cos, by_sin = tables(q_gain)
    k_table[0] = by_cos
    k_table[1] = by_sin
    score_scale = math.log2(math.e) / math.sqrt(width)
    for h in range(heads):
        if h == 0:
            send_own_keys()
        q = ready(q_in[:, h * width : (h + 1) * width], k_table[0], k_table[1])
        q = q.astype(f32) * score_scale
        high = q.astype(bf16)
        low = (q - high.astype(f32)).astype(bf16)
        at = (h % group) * shard_rows
        q_wide[h // group, at : at + shard_rows, :width] = high
        q_wide[h // group, at : at + shard_rows, width:] = low

    def relay(pair):
        block = 2 * pair + side

        to_up(block, VALUES).wait_recv()

        @pl.when(not_last)
        def _():
            to_up(block, VALUES).start()

        to_over(block, VALUES).start()

        to_up(block, KEYS).wait_recv()

        @pl.when(not_last)
        def _():
            to_up(block, KEYS).start()

        @pl.when(pair > 0)
        def _():
            to_over(block, KEYS).start()

    def detour():
        @pl.when(not_first)
        def _():
            to_up(1 - side, KEYS).wait_recv()

        @pl.when(level == 0)
        def _():
            to_over(1 - side, KEYS).wait_recv()

        @pl.when(not_last)
        def _():
            to_up(side, KEYS).wait_send()
            to_up(1 - side, KEYS).start()

    def finish(h, i, o):
        row = lax.broadcasted_iota(jnp.int32, (shard_rows, width), 0)
        for n in range(batch):
            done = o[n * shard_rows : (n + 1) * shard_rows]
            done = jnp.where(row < counts[me], done, 0.0).astype(bf16)
            done_at = slice((i * batch + n) * width, (i * batch + n + 1) * width)
            result[h, :, done_at] = done

    def leave(h):
        part = group * width
        return pltpu.make_async_copy(
            result.at[h],
            out.at[:, pl.ds(pl.multiple_of(h * part, part), part)],
            leaving.at[h],
        )

    def attend(pair, first, last=False):
        blocks = [2 * pair, 2 * pair + 1]
        row = lax.broadcasted_iota(jnp.int32, (shard_rows, width), 0)
        alive = jnp.concatenate(
            [jnp.where(row < counts[b], 1.0, 0.0).astype(bf16) for b in blocks], 0
        )
        if first:
            q_at = lax.broadcasted_iota(jnp.int32, (shard_rows, pair_rows), 0)
            k_at = lax.broadcasted_iota(jnp.int32, (shard_rows, pair_rows), 1)
            seen = k_at <= q_at + side * shard_rows
            seen = jnp.concatenate([seen] * batch, 0) if batch > 1 else seen

        @pl.loop(0, kv_heads)
        def _(h):
            cut = pl.ds(pl.multiple_of(h * width, width), width)
            k = kv[pair, KEYS, :, cut]
            v = kv[pair, VALUES, :, cut] * alive
            k2 = jnp.concatenate([k, k], 1)
            v2 = jnp.concatenate([v, alive], 1)
            rows = batch * shard_rows

            def scores(i):
                q = q_wide[h, pl.ds(i * rows, rows), :]
                return lax.dot_general(
                    q, k2, (((1,), (1,)), ((), ())), preferred_element_type=f32
                )

            steps = group // batch
            coming = scores(0)
            for i in range(steps):
                s = coming
                if i + 1 < steps:
                    coming = scores(i + 1)
                if first:
                    s = jnp.where(seen, s, FAR)
                parts = [s[:, j : j + width] for j in range(0, pair_rows, width)]
                peak = functools.reduce(jnp.maximum, parts)
                peak = jnp.max(peak, -1, keepdims=True)
                state = (h, slice(i * rows, (i + 1) * rows))
                if first:
                    new = jnp.broadcast_to(peak, (rows, width))
                else:
                    old = top[state]
                    new = jnp.maximum(old, peak)
                weights = jnp.concatenate(
                    [jnp.exp2(part - new).astype(bf16) for part in parts], 1
                )
                o = jnp.dot(weights, v2, preferred_element_type=f32)
                if last:
                    rescale = jnp.exp2(old - new)
                    over_total = 1.0 / (total[state] * rescale + o[:, width:])
                    o = (summed[state] * rescale + o[:, :width]) * over_total
                    finish(h, i, o)
                    continue
                top[state] = new
                if first:
                    summed[state] = o[:, :width]
                    total[state] = o[:, width:]
                else:
                    rescale = jnp.exp2(old - new)
                    summed[state] = summed[state] * rescale + o[:, :width]
                    total[state] = total[state] * rescale + o[:, width:]

            if last:
                leave(h).start()

    def await_over(pair):
        block = 2 * pair + 1 - side

        @pl.when(pair > 0)
        def _():
            to_over(block, KEYS).wait_recv()

        to_over(block, VALUES).wait_recv()

    @pl.when(not_first)
    def _():
        relay(level - 1)

    @pl.when(level == 0)
    def _():
        detour()

    @pl.when(side == 1)
    def _():
        @pl.when(not_first)
        def _():
            to_over(me - 1, KEYS).wait_recv()

        to_over(me - 1, VALUES).wait_recv()

    fetches[7].wait()
    attend(level, True)

    @pl.loop(0, level - 1)
    def _(step):
        pair = level - 1 - step
        relay(pair - 1)
        await_over(pair)
        attend(pair, False)

    @pl.when(not_first)
    def _():
        detour()
        await_over(0)
        attend(0, False, True)

    @pl.when(level == 0)
    def _():
        @pl.loop(0, kv_heads)
        def _(h):
            for i in range(group // batch):
                state = (h, slice(i * batch * shard_rows, (i + 1) * batch * shard_rows))
                finish(h, i, summed[state] * (1.0 / total[state]))
            leave(h).start()

    for h in range(kv_heads):
        leave(h).wait()

    @pl.when(side == 0)
    def _():
        to_over(me, VALUES).wait_send()

    @pl.when((side == 0) | (level == 0))
    def _():
        to_over(me, KEYS).wait_send()

    @pl.when(not_last)
    def _():
        to_up(me, VALUES).wait_send()
        to_up(1 - side, KEYS).wait_send()

        @pl.when(not_first)
        def _():
            to_up(me, KEYS).wait_send()

    @pl.loop(0, level)
    def _(pair):
        block = 2 * pair + side
        to_over(block, VALUES).wait_send()

        @pl.when(pair > 0)
        def _():
            to_over(block, KEYS).wait_send()

        @pl.when(not_last)
        def _():
            to_up(block, VALUES).wait_send()

            @pl.when(pair > 0)
            def _():
                to_up(block, KEYS).wait_send()


def local(shards, queries, keys, values, q_gain, k_gain, counts):
    shard_rows = queries.shape[0]
    width = q_gain.shape[0]
    heads = queries.shape[1] // width
    inner, start = rope_constants(shards, shard_rows, width)
    hbm = pl.BlockSpec(memory_space=pl.ANY)
    kv_heads = keys.shape[1] // width
    rows = heads // kv_heads * shard_rows
    state = pltpu.VMEM((kv_heads, rows, width), jnp.float32)
    return pl.pallas_call(
        functools.partial(kernel, shards, width),
        out_shape=jax.ShapeDtypeStruct(queries.shape, jnp.bfloat16),
        in_specs=[hbm] * 8,
        out_specs=hbm,
        scratch_shapes=[
            pltpu.VMEM(queries.shape, jnp.bfloat16),
            pltpu.VMEM(keys.shape, jnp.bfloat16),
            pltpu.VMEM((1, width), jnp.float32),
            pltpu.VMEM((1, width), jnp.float32),
            pltpu.SMEM(counts.shape, jnp.int32),
            pltpu.VMEM(inner.shape, jnp.float32),
            pltpu.VMEM(start.shape[1:], jnp.float32),
            pltpu.VMEM((shards // 2, 2, 2 * shard_rows, keys.shape[1]), jnp.bfloat16),
            pltpu.VMEM((kv_heads, rows, 2 * width), jnp.bfloat16),
            state,
            state,
            state,
            pltpu.VMEM((2, shard_rows, width), jnp.float32),
            pltpu.SemaphoreType.DMA((shards, 2)),
            pltpu.SemaphoreType.DMA((shards, 2)),
            pltpu.SemaphoreType.DMA((shards, 2)),
            pltpu.SemaphoreType.DMA((8,)),
            pltpu.VMEM((kv_heads, shard_rows, queries.shape[1] // kv_heads), jnp.bfloat16),
            pltpu.SemaphoreType.DMA((kv_heads,)),
        ],
        compiler_params=pltpu.CompilerParams(
            collective_id=0, has_side_effects=True, vmem_limit_bytes=60 * 2**20
        ),
        name="attend",
    )(
        queries,
        keys,
        values,
        q_gain.reshape(1, width),
        k_gain.reshape(1, width),
        counts,
        jnp.asarray(inner),
        jnp.asarray(start),
    )


def solution(mesh):
    in_specs = (
        P(("groups", "ctx"), "tp"),
        P(("groups", "ctx"), "tp"),
        P(("groups", "ctx"), "tp"),
        P(),
        P(),
        P("groups"),
    )
    out_specs = P(("groups", "ctx"), "tp")
    return jax.shard_map(
        functools.partial(local, mesh.shape["ctx"]),
        mesh=mesh,
        in_specs=in_specs,
        out_specs=out_specs,
        check_vma=False,
    )
```

```python
import functools
import math

import jax
import jax.numpy as jnp
import numpy as np
from jax import lax
from jax.experimental import pallas as pl
from jax.experimental.pallas import tpu as pltpu
from jax.sharding import PartitionSpec as P

KEYS, VALUES = 0, 1
MESH = pl.DeviceIdType.MESH
FAR = -1e30
THETA = 1000000.0
ROWS = 384


def rope_constants(shards, shard_rows, width):
    frequency = THETA ** (-np.arange(0, width, 2, dtype=np.float64) / width)
    frequency = np.concatenate([frequency, frequency])
    inner = np.arange(shard_rows)[:, None] * frequency[None, :]
    start = (np.arange(shards) * shard_rows)[:, None] * frequency[None, :]
    inner = np.stack([np.cos(inner), np.sin(inner)]).astype(np.float32)
    start = np.stack([np.cos(start), np.sin(start)], 1).astype(np.float32)
    return inner, start


def kernel(
    shards,
    width,
    q_hbm,
    k_hbm,
    v_hbm,
    q_gain_hbm,
    k_gain_hbm,
    counts_hbm,
    inner_hbm,
    start_hbm,
    out,
    q_in,
    k_in,
    q_gain,
    k_gain,
    counts,
    inner,
    start,
    kv,
    q_wide,
    top,
    total,
    summed,
    k_table,
    send_up,
    send_over,
    recv,
    fetched,
):
    shard_rows = q_in.shape[0]
    heads = q_in.shape[1] // width
    kv_heads = k_in.shape[1] // width
    group = heads // kv_heads
    pair_rows = 2 * shard_rows
    levels = shards // 2
    batch = max(1, min(group, ROWS // shard_rows))
    half = width // 2
    bf16, f32 = jnp.bfloat16, jnp.float32

    me = lax.axis_index("ctx")
    level = me // 2
    side = lax.rem(me, 2)
    over = me + 1 - 2 * side
    up = lax.rem(me + 2, shards)
    down = lax.rem(me - 2 + shards, shards)
    not_last = level < levels - 1
    not_first = level > 0
    own = pl.multiple_of(side * shard_rows, shard_rows)

    fetches = [
        pltpu.make_async_copy(source, target, fetched.at[i])
        for i, (source, target) in enumerate(
            [
                (k_hbm, k_in),
                (inner_hbm, inner),
                (start_hbm.at[me], start),
                (k_gain_hbm, k_gain),
                (counts_hbm, counts),
                (q_gain_hbm, q_gain),
                (q_hbm, q_in),
                (v_hbm, kv.at[level, VALUES, pl.ds(own, shard_rows), :]),
            ]
        )
    ]
    for fetch in fetches:
        fetch.start()

    barrier = pltpu.get_barrier_semaphore()
    pl.semaphore_signal(barrier, inc=1, device_id={"ctx": over}, device_id_type=MESH)

    @pl.when(not_last)
    def _():
        pl.semaphore_signal(barrier, inc=1, device_id={"ctx": up}, device_id_type=MESH)

    @pl.when(not_first)
    def _():
        pl.semaphore_signal(barrier, inc=1, device_id={"ctx": down}, device_id_type=MESH)

    def place(block, part):
        offset = pl.multiple_of(lax.rem(block, 2) * shard_rows, shard_rows)
        return kv.at[block // 2, part, pl.ds(offset, shard_rows), :]

    def copy(block, part, sems, target, source):
        return pltpu.make_async_remote_copy(
            src_ref=place(block, part) if source is None else source,
            dst_ref=place(block, part),
            send_sem=sems.at[block, part],
            recv_sem=recv.at[block, part],
            device_id={"ctx": target},
            device_id_type=MESH,
        )

    def to_up(block, part, source=None):
        return copy(block, part, send_up, up, source)

    def to_over(block, part, source=None):
        return copy(block, part, send_over, over, source)

    pl.semaphore_wait(
        barrier, 1 + jnp.where(not_last, 1, 0) + jnp.where(not_first, 1, 0)
    )

    @pl.when(side == 0)
    def _():
        to_over(me, VALUES, v_hbm).start()

    @pl.when(not_last)
    def _():
        to_up(me, VALUES, v_hbm).start()

    def send_own_keys():
        @pl.when((side == 0) | (level == 0))
        def _():
            to_over(me, KEYS).start()

        @pl.when(not_last)
        def _():
            to_up(me, KEYS).start()

    for fetch in fetches[:5]:
        fetch.wait()
    c0 = start[0:1, :]
    s0 = start[1:2, :]
    ci = inner[0]
    si = inner[1]
    cosine = c0 * ci - s0 * si
    sine = s0 * ci + c0 * si
    lane = lax.broadcasted_iota(jnp.int32, (1, width), 1)
    sine = jnp.where(lane < half, -sine, sine)

    def tables(gain):
        g = gain[...]
        return cosine * g, sine * pltpu.roll(g, half, 1)

    def ready(x, by_cos, by_sin):
        x = x.astype(f32)
        scale = lax.rsqrt(jnp.mean(x * x, -1, keepdims=True) + 1e-06)
        return ((x * by_cos + pltpu.roll(x, half, 1) * by_sin) * scale).astype(bf16)

    live = lax.broadcasted_iota(jnp.int32, (shard_rows, width), 0) < counts[me]
    by_cos, by_sin = tables(k_gain)
    for h in range(kv_heads):
        cut = slice(h * width, (h + 1) * width)
        k = ready(k_in[:, cut], by_cos, by_sin).astype(f32)
        k = jnp.where(live, k, k[0:1, :])
        kv[level, KEYS, pl.ds(own, shard_rows), cut] = k.astype(bf16)

    @pl.when(side == 0)
    def _():
        blank = jnp.zeros((shard_rows, kv_heads * width), bf16)
        kv[level, VALUES, shard_rows:, :] = blank

        @pl.when(not_first)
        def _():
            kv[level, KEYS, shard_rows:, :] = blank

    for fetch in fetches[5:7]:
        fetch.wait()
    by_cos, by_sin = tables(q_gain)
    k_table[0] = by_cos
    k_table[1] = by_sin
    score_scale = math.log2(math.e) / math.sqrt(width)
    for h in range(heads):
        if h == 0:
            send_own_keys()
        q = ready(q_in[:, h * width : (h + 1) * width], k_table[0], k_table[1])
        q = q.astype(f32) * score_scale
        high = q.astype(bf16)
        low = (q - high.astype(f32)).astype(bf16)
        at = (h % group) * shard_rows
        q_wide[h // group, at : at + shard_rows, :width] = high
        q_wide[h // group, at : at + shard_rows, width:] = low

    def relay(pair):
        block = 2 * pair + side

        to_up(block, VALUES).wait_recv()

        @pl.when(not_last)
        def _():
            to_up(block, VALUES).start()

        to_over(block, VALUES).start()

        to_up(block, KEYS).wait_recv()

        @pl.when(not_last)
        def _():
            to_up(block, KEYS).start()

        @pl.when(pair > 0)
        def _():
            to_over(block, KEYS).start()

    def detour():
        @pl.when(not_first)
        def _():
            to_up(1 - side, KEYS).wait_recv()

        @pl.when(level == 0)
        def _():
            to_over(1 - side, KEYS).wait_recv()

        @pl.when(not_last)
        def _():
            to_up(side, KEYS).wait_send()
            to_up(1 - side, KEYS).start()

    def finish(h, i, o):
        row = lax.broadcasted_iota(jnp.int32, (shard_rows, width), 0)
        for n in range(batch):
            done = o[n * shard_rows : (n + 1) * shard_rows]
            done = jnp.where(row < counts[me], done, 0.0).astype(bf16)
            at = pl.multiple_of((h * group + i * batch + n) * width, width)
            out[:, pl.ds(at, width)] = done

    def attend(pair, first, last=False):
        blocks = [2 * pair, 2 * pair + 1]
        row = lax.broadcasted_iota(jnp.int32, (shard_rows, width), 0)
        alive = jnp.concatenate(
            [jnp.where(row < counts[b], 1.0, 0.0).astype(bf16) for b in blocks], 0
        )
        if first:
            q_at = lax.broadcasted_iota(jnp.int32, (shard_rows, pair_rows), 0)
            k_at = lax.broadcasted_iota(jnp.int32, (shard_rows, pair_rows), 1)
            seen = k_at <= q_at + side * shard_rows
            seen = jnp.concatenate([seen] * batch, 0) if batch > 1 else seen

        @pl.loop(0, kv_heads)
        def _(h):
            cut = pl.ds(pl.multiple_of(h * width, width), width)
            k = kv[pair, KEYS, :, cut]
            v = kv[pair, VALUES, :, cut] * alive
            k2 = jnp.concatenate([k, k], 1)
            v2 = jnp.concatenate([v, alive], 1)
            rows = batch * shard_rows

            def scores(i):
                q = q_wide[h, pl.ds(i * rows, rows), :]
                return lax.dot_general(
                    q, k2, (((1,), (1,)), ((), ())), preferred_element_type=f32
                )

            steps = group // batch
            coming = scores(0)
            for i in range(steps):
                s = coming
                if i + 1 < steps:
                    coming = scores(i + 1)
                if first:
                    s = jnp.where(seen, s, FAR)
                parts = [s[:, j : j + width] for j in range(0, pair_rows, width)]
                peak = functools.reduce(jnp.maximum, parts)
                peak = jnp.max(peak, -1, keepdims=True)
                state = (h, slice(i * rows, (i + 1) * rows))
                if first:
                    new = jnp.broadcast_to(peak, (rows, width))
                else:
                    old = top[state]
                    new = jnp.maximum(old, peak)
                weights = jnp.concatenate(
                    [jnp.exp2(part - new).astype(bf16) for part in parts], 1
                )
                o = jnp.dot(weights, v2, preferred_element_type=f32)
                if last:
                    rescale = jnp.exp2(old - new)
                    over_total = 1.0 / (total[state] * rescale + o[:, width:])
                    o = (summed[state] * rescale + o[:, :width]) * over_total
                    finish(h, i, o)
                    continue
                top[state] = new
                if first:
                    summed[state] = o[:, :width]
                    total[state] = o[:, width:]
                else:
                    rescale = jnp.exp2(old - new)
                    summed[state] = summed[state] * rescale + o[:, :width]
                    total[state] = total[state] * rescale + o[:, width:]

    def await_over(pair):
        block = 2 * pair + 1 - side

        @pl.when(pair > 0)
        def _():
            to_over(block, KEYS).wait_recv()

        to_over(block, VALUES).wait_recv()

    @pl.when(not_first)
    def _():
        relay(level - 1)

    @pl.when(level == 0)
    def _():
        detour()

    @pl.when(side == 1)
    def _():
        @pl.when(not_first)
        def _():
            to_over(me - 1, KEYS).wait_recv()

        to_over(me - 1, VALUES).wait_recv()

    fetches[7].wait()
    attend(level, True)

    @pl.loop(0, level - 1)
    def _(step):
        pair = level - 1 - step
        relay(pair - 1)
        await_over(pair)
        attend(pair, False)

    @pl.when(not_first)
    def _():
        detour()
        await_over(0)
        attend(0, False, True)

    @pl.when(level == 0)
    def _():
        @pl.loop(0, kv_heads)
        def _(h):
            for i in range(group // batch):
                state = (h, slice(i * batch * shard_rows, (i + 1) * batch * shard_rows))
                finish(h, i, summed[state] * (1.0 / total[state]))

    @pl.when(side == 0)
    def _():
        to_over(me, VALUES).wait_send()

    @pl.when((side == 0) | (level == 0))
    def _():
        to_over(me, KEYS).wait_send()

    @pl.when(not_last)
    def _():
        to_up(me, VALUES).wait_send()
        to_up(1 - side, KEYS).wait_send()

        @pl.when(not_first)
        def _():
            to_up(me, KEYS).wait_send()

    @pl.loop(0, level)
    def _(pair):
        block = 2 * pair + side
        to_over(block, VALUES).wait_send()

        @pl.when(pair > 0)
        def _():
            to_over(block, KEYS).wait_send()

        @pl.when(not_last)
        def _():
            to_up(block, VALUES).wait_send()

            @pl.when(pair > 0)
            def _():
                to_up(block, KEYS).wait_send()


def local(shards, queries, keys, values, q_gain, k_gain, counts):
    shard_rows = queries.shape[0]
    width = q_gain.shape[0]
    heads = queries.shape[1] // width
    inner, start = rope_constants(shards, shard_rows, width)
    hbm = pl.BlockSpec(memory_space=pl.ANY)
    kv_heads = keys.shape[1] // width
    rows = heads // kv_heads * shard_rows
    state = pltpu.VMEM((kv_heads, rows, width), jnp.float32)
    return pl.pallas_call(
        functools.partial(kernel, shards, width),
        out_shape=pltpu.VMEM(queries.shape, jnp.bfloat16),
        in_specs=[hbm] * 8,
        out_specs=pl.BlockSpec(memory_space=pltpu.VMEM),
        scratch_shapes=[
            pltpu.VMEM(queries.shape, jnp.bfloat16),
            pltpu.VMEM(keys.shape, jnp.bfloat16),
            pltpu.VMEM((1, width), jnp.float32),
            pltpu.VMEM((1, width), jnp.float32),
            pltpu.SMEM(counts.shape, jnp.int32),
            pltpu.VMEM(inner.shape, jnp.float32),
            pltpu.VMEM(start.shape[1:], jnp.float32),
            pltpu.VMEM((shards // 2, 2, 2 * shard_rows, keys.shape[1]), jnp.bfloat16),
            pltpu.VMEM((kv_heads, rows, 2 * width), jnp.bfloat16),
            state,
            state,
            state,
            pltpu.VMEM((2, shard_rows, width), jnp.float32),
            pltpu.SemaphoreType.DMA((shards, 2)),
            pltpu.SemaphoreType.DMA((shards, 2)),
            pltpu.SemaphoreType.DMA((shards, 2)),
            pltpu.SemaphoreType.DMA((8,)),
        ],
        compiler_params=pltpu.CompilerParams(
            collective_id=0, has_side_effects=True, vmem_limit_bytes=60 * 2**20
        ),
        name="attend",
    )(
        queries,
        keys,
        values,
        q_gain.reshape(1, width),
        k_gain.reshape(1, width),
        counts,
        jnp.asarray(inner),
        jnp.asarray(start),
    )


def solution(mesh):
    in_specs = (
        P(("groups", "ctx"), "tp"),
        P(("groups", "ctx"), "tp"),
        P(("groups", "ctx"), "tp"),
        P(),
        P(),
        P("groups"),
    )
    out_specs = P(("groups", "ctx"), "tp")
    return jax.shard_map(
        functools.partial(local, mesh.shape["ctx"]),
        mesh=mesh,
        in_specs=in_specs,
        out_specs=out_specs,
        check_vma=False,
    )
```

```python
import functools
import math

import jax
import jax.numpy as jnp
import numpy as np
from jax import lax
from jax.experimental import pallas as pl
from jax.experimental.pallas import tpu as pltpu
from jax.sharding import PartitionSpec as P

KEYS, VALUES = 0, 1
MESH = pl.DeviceIdType.MESH
FAR = -1e30
THETA = 1000000.0
ROWS = 384


def rope_constants(shards, shard_rows, width):
    frequency = THETA ** (-np.arange(0, width, 2, dtype=np.float64) / width)
    frequency = np.concatenate([frequency, frequency])
    inner = np.arange(shard_rows)[:, None] * frequency[None, :]
    start = (np.arange(shards) * shard_rows)[:, None] * frequency[None, :]
    inner = np.stack([np.cos(inner), np.sin(inner)]).astype(np.float32)
    start = np.stack([np.cos(start), np.sin(start)], 1).astype(np.float32)
    return inner, start


def kernel(
    shards,
    width,
    q_hbm,
    k_hbm,
    v_hbm,
    q_gain_hbm,
    k_gain_hbm,
    counts_hbm,
    inner_hbm,
    start_hbm,
    out,
    q_in,
    k_in,
    q_gain,
    k_gain,
    counts,
    inner,
    start,
    kv,
    q_wide,
    top,
    total,
    summed,
    k_table,
    send_up,
    send_over,
    recv,
    fetched,
):
    shard_rows = q_in.shape[0]
    heads = q_in.shape[1] // width
    kv_heads = k_in.shape[1] // width
    group = heads // kv_heads
    pair_rows = 2 * shard_rows
    levels = shards // 2
    batch = max(1, min(group, ROWS // shard_rows))
    half = width // 2
    bf16, f32 = jnp.bfloat16, jnp.float32

    me = lax.axis_index("ctx")
    level = me // 2
    side = lax.rem(me, 2)
    over = me + 1 - 2 * side
    up = lax.rem(me + 2, shards)
    down = lax.rem(me - 2 + shards, shards)
    not_last = level < levels - 1
    not_first = level > 0
    own = pl.multiple_of(side * shard_rows, shard_rows)

    fetches = [
        pltpu.make_async_copy(source, target, fetched.at[i])
        for i, (source, target) in enumerate(
            [
                (k_hbm, k_in),
                (inner_hbm, inner),
                (start_hbm.at[me], start),
                (k_gain_hbm, k_gain),
                (counts_hbm, counts),
                (q_gain_hbm, q_gain),
                (q_hbm, q_in),
                (v_hbm, kv.at[level, VALUES, pl.ds(own, shard_rows), :]),
            ]
        )
    ]
    for fetch in fetches:
        fetch.start()

    barrier = pltpu.get_barrier_semaphore()
    pl.semaphore_signal(barrier, inc=1, device_id={"ctx": over}, device_id_type=MESH)

    @pl.when(not_last)
    def _():
        pl.semaphore_signal(barrier, inc=1, device_id={"ctx": up}, device_id_type=MESH)

    @pl.when(not_first)
    def _():
        pl.semaphore_signal(barrier, inc=1, device_id={"ctx": down}, device_id_type=MESH)

    def place(block, part):
        offset = pl.multiple_of(lax.rem(block, 2) * shard_rows, shard_rows)
        return kv.at[block // 2, part, pl.ds(offset, shard_rows), :]

    def copy(block, part, sems, target, source):
        return pltpu.make_async_remote_copy(
            src_ref=place(block, part) if source is None else source,
            dst_ref=place(block, part),
            send_sem=sems.at[block, part],
            recv_sem=recv.at[block, part],
            device_id={"ctx": target},
            device_id_type=MESH,
        )

    def to_up(block, part, source=None):
        return copy(block, part, send_up, up, source)

    def to_over(block, part, source=None):
        return copy(block, part, send_over, over, source)

    pl.semaphore_wait(
        barrier, 1 + jnp.where(not_last, 1, 0) + jnp.where(not_first, 1, 0)
    )

    @pl.when(side == 0)
    def _():
        to_over(me, VALUES, v_hbm).start()

    @pl.when(not_last)
    def _():
        to_up(me, VALUES, v_hbm).start()

    def send_own_keys():
        @pl.when((side == 0) | (level == 0))
        def _():
            to_over(me, KEYS).start()

        @pl.when(not_last)
        def _():
            to_up(me, KEYS).start()

    for fetch in fetches[:5]:
        fetch.wait()
    c0 = start[0:1, :]
    s0 = start[1:2, :]
    ci = inner[0]
    si = inner[1]
    cosine = c0 * ci - s0 * si
    sine = s0 * ci + c0 * si
    lane = lax.broadcasted_iota(jnp.int32, (1, width), 1)
    sine = jnp.where(lane < half, -sine, sine)

    def tables(gain):
        g = gain[...]
        return cosine * g, sine * pltpu.roll(g, half, 1)

    def ready(x, by_cos, by_sin):
        x = x.astype(f32)
        scale = lax.rsqrt(jnp.mean(x * x, -1, keepdims=True) + 1e-06)
        return ((x * by_cos + pltpu.roll(x, half, 1) * by_sin) * scale).astype(bf16)

    live = lax.broadcasted_iota(jnp.int32, (shard_rows, width), 0) < counts[me]
    by_cos, by_sin = tables(k_gain)
    for h in range(kv_heads):
        cut = slice(h * width, (h + 1) * width)
        k = ready(k_in[:, cut], by_cos, by_sin).astype(f32)
        k = jnp.where(live, k, k[0:1, :])
        kv[level, KEYS, pl.ds(own, shard_rows), cut] = k.astype(bf16)

    @pl.when(side == 0)
    def _():
        blank = jnp.zeros((shard_rows, kv_heads * width), bf16)
        kv[level, VALUES, shard_rows:, :] = blank

        @pl.when(not_first)
        def _():
            kv[level, KEYS, shard_rows:, :] = blank

    for fetch in fetches[5:7]:
        fetch.wait()
    by_cos, by_sin = tables(q_gain)
    k_table[0] = by_cos
    k_table[1] = by_sin
    score_scale = math.log2(math.e) / math.sqrt(width)
    for h in range(heads):
        if h == 0:
            send_own_keys()
        q = ready(q_in[:, h * width : (h + 1) * width], k_table[0], k_table[1])
        q = q.astype(f32) * score_scale
        high = q.astype(bf16)
        low = (q - high.astype(f32)).astype(bf16)
        at = (h % group) * shard_rows
        q_wide[h // group, at : at + shard_rows, :width] = high
        q_wide[h // group, at : at + shard_rows, width:] = low

    def relay(pair):
        block = 2 * pair + side

        to_up(block, VALUES).wait_recv()

        @pl.when(not_last)
        def _():
            to_up(block, VALUES).start()

        to_over(block, VALUES).start()

        @pl.when(not_last | (pair > 0))
        def _():
            to_up(block, KEYS).wait_recv()

        @pl.when(not_last)
        def _():
            to_up(block, KEYS).start()

        @pl.when(pair > 0)
        def _():
            to_over(block, KEYS).start()

    def detour():
        @pl.when(not_first)
        def _():
            to_up(1 - side, KEYS).wait_recv()

        @pl.when(level == 0)
        def _():
            to_over(1 - side, KEYS).wait_recv()

        @pl.when(not_last)
        def _():
            to_up(side, KEYS).wait_send()
            to_up(1 - side, KEYS).start()

    def finish(h, i, o):
        row = lax.broadcasted_iota(jnp.int32, (shard_rows, width), 0)
        for n in range(batch):
            done = o[n * shard_rows : (n + 1) * shard_rows]
            done = jnp.where(row < counts[me], done, 0.0).astype(bf16)
            at = pl.multiple_of((h * group + i * batch + n) * width, width)
            out[:, pl.ds(at, width)] = done

    def attend(pair, first, last=False):
        blocks = [2 * pair, 2 * pair + 1]
        row = lax.broadcasted_iota(jnp.int32, (shard_rows, width), 0)
        alive = jnp.concatenate(
            [jnp.where(row < counts[b], 1.0, 0.0).astype(bf16) for b in blocks], 0
        )
        if first:
            q_at = lax.broadcasted_iota(jnp.int32, (shard_rows, pair_rows), 0)
            k_at = lax.broadcasted_iota(jnp.int32, (shard_rows, pair_rows), 1)
            seen = k_at <= q_at + side * shard_rows
            seen = jnp.concatenate([seen] * batch, 0) if batch > 1 else seen

        @pl.loop(0, kv_heads)
        def _(h):
            cut = pl.ds(pl.multiple_of(h * width, width), width)
            k = kv[pair, KEYS, :, cut]
            v = kv[pair, VALUES, :, cut] * alive
            k2 = jnp.concatenate([k, k], 1)
            v2 = jnp.concatenate([v, alive], 1)
            rows = batch * shard_rows

            def scores(i):
                q = q_wide[h, pl.ds(i * rows, rows), :]
                return lax.dot_general(
                    q, k2, (((1,), (1,)), ((), ())), preferred_element_type=f32
                )

            steps = group // batch
            coming = scores(0)
            for i in range(steps):
                s = coming
                if i + 1 < steps:
                    coming = scores(i + 1)
                if first:
                    s = jnp.where(seen, s, FAR)
                parts = [s[:, j : j + width] for j in range(0, pair_rows, width)]
                peak = functools.reduce(jnp.maximum, parts)
                peak = jnp.max(peak, -1, keepdims=True)
                state = (h, slice(i * rows, (i + 1) * rows))
                if first:
                    new = jnp.broadcast_to(peak, (rows, width))
                else:
                    old = top[state]
                    new = jnp.maximum(old, peak)
                weights = jnp.concatenate(
                    [jnp.exp2(part - new).astype(bf16) for part in parts], 1
                )
                o = jnp.dot(weights, v2, preferred_element_type=f32)
                if last:
                    rescale = jnp.exp2(old - new)
                    over_total = 1.0 / (total[state] * rescale + o[:, width:])
                    o = (summed[state] * rescale + o[:, :width]) * over_total
                    finish(h, i, o)
                    continue
                top[state] = new
                if first:
                    summed[state] = o[:, :width]
                    total[state] = o[:, width:]
                else:
                    rescale = jnp.exp2(old - new)
                    summed[state] = summed[state] * rescale + o[:, :width]
                    total[state] = total[state] * rescale + o[:, width:]

    def await_over(pair):
        block = 2 * pair + 1 - side

        @pl.when(pair > 0)
        def _():
            to_over(block, KEYS).wait_recv()

        to_over(block, VALUES).wait_recv()

    @pl.when(not_first)
    def _():
        relay(level - 1)

    @pl.when(level == 0)
    def _():
        detour()

    @pl.when(side == 1)
    def _():
        @pl.when(not_first)
        def _():
            to_over(me - 1, KEYS).wait_recv()

        to_over(me - 1, VALUES).wait_recv()

    fetches[7].wait()
    attend(level, True)

    @pl.loop(0, level - 1)
    def _(step):
        pair = level - 1 - step
        relay(pair - 1)
        await_over(pair)
        attend(pair, False)

    @pl.when(not_first)
    def _():
        @pl.when(level == levels - 1)
        def _():
            to_up(side, KEYS).wait_recv()

        detour()
        await_over(0)
        attend(0, False, True)

    @pl.when(level == 0)
    def _():
        @pl.loop(0, kv_heads)
        def _(h):
            for i in range(group // batch):
                state = (h, slice(i * batch * shard_rows, (i + 1) * batch * shard_rows))
                finish(h, i, summed[state] * (1.0 / total[state]))

    @pl.when(side == 0)
    def _():
        to_over(me, VALUES).wait_send()

    @pl.when((side == 0) | (level == 0))
    def _():
        to_over(me, KEYS).wait_send()

    @pl.when(not_last)
    def _():
        to_up(me, VALUES).wait_send()
        to_up(1 - side, KEYS).wait_send()

        @pl.when(not_first)
        def _():
            to_up(me, KEYS).wait_send()

    @pl.loop(0, level)
    def _(pair):
        block = 2 * pair + side
        to_over(block, VALUES).wait_send()

        @pl.when(pair > 0)
        def _():
            to_over(block, KEYS).wait_send()

        @pl.when(not_last)
        def _():
            to_up(block, VALUES).wait_send()

            @pl.when(pair > 0)
            def _():
                to_up(block, KEYS).wait_send()


def local(shards, queries, keys, values, q_gain, k_gain, counts):
    shard_rows = queries.shape[0]
    width = q_gain.shape[0]
    heads = queries.shape[1] // width
    inner, start = rope_constants(shards, shard_rows, width)
    hbm = pl.BlockSpec(memory_space=pl.ANY)
    kv_heads = keys.shape[1] // width
    rows = heads // kv_heads * shard_rows
    state = pltpu.VMEM((kv_heads, rows, width), jnp.float32)
    return pl.pallas_call(
        functools.partial(kernel, shards, width),
        out_shape=pltpu.VMEM(queries.shape, jnp.bfloat16),
        in_specs=[hbm] * 8,
        out_specs=pl.BlockSpec(memory_space=pltpu.VMEM),
        scratch_shapes=[
            pltpu.VMEM(queries.shape, jnp.bfloat16),
            pltpu.VMEM(keys.shape, jnp.bfloat16),
            pltpu.VMEM((1, width), jnp.float32),
            pltpu.VMEM((1, width), jnp.float32),
            pltpu.SMEM(counts.shape, jnp.int32),
            pltpu.VMEM(inner.shape, jnp.float32),
            pltpu.VMEM(start.shape[1:], jnp.float32),
            pltpu.VMEM((shards // 2, 2, 2 * shard_rows, keys.shape[1]), jnp.bfloat16),
            pltpu.VMEM((kv_heads, rows, 2 * width), jnp.bfloat16),
            state,
            state,
            state,
            pltpu.VMEM((2, shard_rows, width), jnp.float32),
            pltpu.SemaphoreType.DMA((shards, 2)),
            pltpu.SemaphoreType.DMA((shards, 2)),
            pltpu.SemaphoreType.DMA((shards, 2)),
            pltpu.SemaphoreType.DMA((8,)),
        ],
        compiler_params=pltpu.CompilerParams(
            collective_id=0, has_side_effects=True, vmem_limit_bytes=60 * 2**20
        ),
        name="attend",
    )(
        queries,
        keys,
        values,
        q_gain.reshape(1, width),
        k_gain.reshape(1, width),
        counts,
        jnp.asarray(inner),
        jnp.asarray(start),
    )


def solution(mesh):
    in_specs = (
        P(("groups", "ctx"), "tp"),
        P(("groups", "ctx"), "tp"),
        P(("groups", "ctx"), "tp"),
        P(),
        P(),
        P("groups"),
    )
    out_specs = P(("groups", "ctx"), "tp")
    return jax.shard_map(
        functools.partial(local, mesh.shape["ctx"]),
        mesh=mesh,
        in_specs=in_specs,
        out_specs=out_specs,
        check_vma=False,
    )
```
